512 devices in a mesh: row: 16 (over z), col: 32 (over y, x, core).
Axes of the slice: x: 4, y: 4, z: 16, core: 2. Of those that a mesh axis runs over, the one named last changes fastest.
Arguments:
- momentum: bfloat16 [8192, 28672], P('row', 'col'), may hold values from -6 to 6
- gradient: bfloat16 [8192, 28672], P('row', 'col'), may hold values from -6 to 6
- basis: bfloat16 [28672, 512], P('col'), may hold values from -6 to 6
Outputs:
- momentum_next: bfloat16 [8192, 28672], P('row', 'col')
- left_basis: float32 [8192, 512], P('row')
- right_basis: float32 [28672, 512], P('col')
The draws below stay inside these ranges and needn't reach their ends.
All inputs are finite; a program needn't handle non-finite values.
Results may differ from the reference program's by a relative error of at most 0.013.
Values sent between devices are 32-bit elements; how exact they have to be, the bound alone decides.
A program may use at most 64 MiB of HBM per device.

```python
import jax
import jax.numpy as jnp
from jax import lax

RANK = 512
ROWS = 8192
COLS = 28672


def shard_levels(key, shape, split, low, high):
    loudness = 1.0
    for dim, blocks in split:
        steps = jax.random.uniform(jax.random.fold_in(jax.random.fold_in(key, 6), dim), (blocks,), jnp.float32, low / len(split), high / len(split))
        loudness = loudness * jnp.repeat(jnp.exp(steps), shape[dim] // blocks).reshape((-1,) + (1,) * (len(shape) - 1 - dim))
    return loudness


def centred(own_key, dims, width, most, pieces=(), kind=jnp.bfloat16):
    factor_of = shard_levels(own_key, dims, pieces, -0.22, 0.18) if pieces else 1.0
    array = jax.random.normal(own_key, dims, jnp.float32) * width * factor_of
    return jnp.minimum(jnp.maximum(array, -most), most).astype(kind)


def setup_inputs(seed: int = 0) -> dict:
    seeds = jax.random.split(jax.random.key(seed), 4)
    momentum = centred(seeds[0], (ROWS, COLS), 1.0, 6.0, ((0, 16), (1, 32)))
    gradient = centred(seeds[1], (ROWS, COLS), 0.5, 6.0, ((0, 16), (1, 32)))
    basis = centred(seeds[2], (COLS, RANK), 1.0, 6.0, ((0, 32),))
    return {"momentum": momentum, "gradient": gradient, "basis": basis}


decay = 0.9

def reference(momentum, gradient, basis):
    buffer = (momentum.astype(jnp.float32) + gradient.astype(jnp.float32)).astype(jnp.bfloat16)
    projected = jnp.dot(buffer.astype(jnp.float32), basis.astype(jnp.float32), preferred_element_type=jnp.float32)
    gram = jnp.dot(projected.T, projected, precision=lax.Precision.HIGHEST)
    lower = jnp.linalg.cholesky(gram)
    orth = jax.scipy.linalg.solve_triangular(lower, projected.T, lower=True).T
    left_basis = jnp.sqrt(jnp.float32(ROWS)) * orth
    orth_half = orth.astype(jnp.bfloat16)
    back = jnp.dot(buffer.T.astype(jnp.float32), orth_half.astype(jnp.float32), preferred_element_type=jnp.float32)
    total = lax.optimization_barrier(jnp.sum(back * back, axis=0))
    right_basis = back * (jnp.sqrt(jnp.float32(COLS)) * lax.rsqrt(total + 1e-06))
    back_half = back.astype(jnp.bfloat16)
    update = jnp.dot(orth_half.astype(jnp.float32), back_half.T.astype(jnp.float32), preferred_element_type=jnp.float32)
    momentum_next = (buffer.astype(jnp.float32) - (1.0 - decay) * update).astype(jnp.bfloat16)
    return (momentum_next, left_basis, right_basis)
```

```python
import jax
import jax.numpy as jnp
from jax import lax
from jax.experimental import pallas as pl
from jax.experimental.pallas import tpu as pltpu
from jax.sharding import PartitionSpec as P

F32 = jnp.float32
BF16 = jnp.bfloat16
MESH = pl.DeviceIdType.MESH
decay = 0.9

NZ, NY, NX = 16, 4, 4
CHIPS = NY * NX
ROWS_L, COLS_L, RANK = 512, 896, 512
CH = 4
LW = RANK // CH
SH = COLS_L // NZ
HALF = ROWS_L // 2
PIECE = HALF // CHIPS
BLOCKS = [(i, j) for i in range(4) for j in range(i + 1)]
TILES = 16 * len(BLOCKS)
OWN = TILES // (2 * CHIPS)
NN = ((1,), (0,))
NT = ((1,), (1,))
TN = ((0,), (0,))


def dot1(a, b, dims):
    return lax.dot_general(a, b, (dims, ((), ())), preferred_element_type=F32)


def doth(a, b, dims):
    return lax.dot_general(a, b, (dims, ((), ())), preferred_element_type=F32, precision=lax.Precision.HIGHEST)


def split(a):
    high = a.astype(BF16)
    return high, (a - high.astype(F32)).astype(BF16)


def splat(a, row, lane):
    return jnp.broadcast_to(a[row : row + 1, lane : lane + 1], (8, 128))


def leaf(a_ref, w_ref, t):
    c0 = 8 * t
    ra = [jnp.broadcast_to(a_ref[c0 + i : c0 + i + 1, :], (8, 128)) for i in range(8)]
    s = {(i, j): jnp.broadcast_to(ra[i][:, c0 + j : c0 + j + 1], (8, 128)) for j in range(8) for i in range(j, 8)}
    rw = [jnp.broadcast_to(w_ref[c0 + i : c0 + i + 1, :], (8, 128)) for i in range(8)]
    low = {}
    r = []
    for k in range(8):
        rk = lax.rsqrt(s[k, k])
        r.append(rk)
        ra[k] = ra[k] * rk
        rw[k] = rw[k] * rk
        for i in range(k + 1, 8):
            low[i, k] = s[i, k] * rk
        for j in range(k + 1, 8):
            for i in range(j, 8):
                s[i, j] = s[i, j] - low[i, k] * low[j, k]
        for i in range(k + 1, 8):
            ra[i] = ra[i] - low[i, k] * ra[k]
            rw[i] = rw[i] - low[i, k] * rw[k]
    sub = lax.broadcasted_iota(jnp.int32, (8, 128), 0)
    wt = rw[0]
    for k in range(1, 8):
        wt = jnp.where(sub == k, rw[k], wt)
    for k in range(7, -1, -1):
        ra[k] = ra[k] * r[k]
        rw[k] = rw[k] * r[k]
        for i in range(k):
            ra[i] = ra[i] - low[k, i] * ra[k]
            rw[i] = rw[i] - low[k, i] * rw[k]
    for i in range(t + 1, 16):
        q = slice(8 * i, 8 * i + 8)
        ai = a_ref[q, :]
        ua = uw = None
        for j in range(8):
            m = jnp.broadcast_to(ai[:, c0 + j : c0 + j + 1], (8, 128))
            ua = m * ra[j] if j == 0 else ua + m * ra[j]
            uw = m * rw[j] if j == 0 else uw + m * rw[j]
        a_ref[q, :] = ai - ua
        w_ref[q, :] = w_ref[q, :] - uw
    w_ref[c0 : c0 + 8, :] = wt


def kernel(
    m_hbm, g_hbm, q_hbm, mom_out, left_out, right_out,
    mv, gv, qv, buf, mt, pp, sibr, rsr, pf, ph, plo, bp,
    rr, rl, bfull, bh, bl, gl, gr, gt, g, li, wd, lh, ll, lf, oh, back, nsq, nr, mn,
    in_s, out_s, s1s, s1r, s2s, s2r, s3s, s3r, s4s, s4r,
    gzs, gzr, gbs, gbr, gps, gpr, gss, gsr,
    ring_s, rsem_r, rsem_l, asem_r, asem_l, ns, nrs,
):
    z = lax.axis_index("row")
    c = lax.axis_index("col")
    y, x, k = c // 8, (c // 2) % 4, c % 2
    chip = y * NX + x
    mine = k * CHIPS + chip

    def dev(zz, yy, xx, kk):
        return (zz, (yy * NX + xx) * 2 + kk)

    def plane(dy, dx, kk):
        return dev(z, (y + dy) % NY, (x + dx) % NX, kk)

    def peer_chip(dy, dx):
        return ((y + dy) % NY) * NX + (x + dx) % NX

    offs = [(dy, dx) for dy in range(NY) for dx in range(NX) if dy or dx]
    sib = dev(z, y, x, 1 - k)
    right_dev = dev((z + 1) % NZ, y, x, k)
    left_dev = dev((z + NZ - 1) % NZ, y, x, k)

    def rcopy(src, dst, ss, rs, device):
        cp = pltpu.make_async_remote_copy(
            src_ref=src, dst_ref=dst, send_sem=ss, recv_sem=rs, device_id=device, device_id_type=MESH
        )
        cp.start()

    def wait_for(ref, sem):
        pltpu.make_async_copy(ref, ref, sem).wait()

    loads = [pltpu.make_async_copy(a, b, in_s.at[i]) for i, (a, b) in enumerate([(m_hbm, mv), (g_hbm, gv), (q_hbm, qv)])]
    for cp in loads:
        cp.start()

    bar = pltpu.get_barrier_semaphore()
    pl.semaphore_signal(bar, inc=1, device_id=sib, device_id_type=MESH)
    for dy, dx in offs:
        for kk in range(2):
            pl.semaphore_signal(bar, inc=1, device_id=plane(dy, dx, kk), device_id_type=MESH)
    for dz in range(1, NZ):
        pl.semaphore_signal(bar, inc=1, device_id=dev((z + dz) % NZ, y, x, k), device_id_type=MESH)

    loads[0].wait()
    loads[1].wait()
    for r in range(4):
        rows = pl.ds(128 * r, 128)
        buf[rows, :] = (mv[rows, :].astype(F32) + gv[rows, :].astype(F32)).astype(BF16)
    loads[2].wait()
    for h in range(2):
        part = dot1(buf[...], qv[:, 256 * h : 256 * h + 256], NN)
        pp[2 * h] = part[:, :128]
        pp[2 * h + 1] = part[:, 128:]

    pl.semaphore_wait(bar, 31 + NZ - 1)

    my_half = pl.multiple_of(HALF * k, HALF)
    other_half = pl.multiple_of(HALF * (1 - k), HALF)
    my_piece = pl.multiple_of(HALF * k + PIECE * chip, PIECE)
    for q in range(CH):
        rcopy(pp.at[q, pl.ds(other_half, HALF)], sibr.at[q], s1s.at[q], s1r.at[q], sib)
    for r in range(4):
        mt[:, 128 * r : 128 * r + 128] = buf[128 * r : 128 * r + 128, :].T
    for q in range(CH):
        wait_for(sibr.at[q], s1r.at[q])
        rows = pl.ds(my_half, HALF)
        pp[q, rows, :] = pp[q, rows, :] + sibr[q]
        for n, (dy, dx) in enumerate(offs):
            piece = pl.multiple_of(HALF * k + PIECE * peer_chip(dy, dx), PIECE)
            rcopy(pp.at[q, pl.ds(piece, PIECE)], rsr.at[q, n], s2s.at[q], s2r.at[q], plane(dy, dx, k))
    for q in range(CH):
        wait_for(rsr.at[q], s2r.at[q])
        rows = pl.ds(my_piece, PIECE)
        total = pp[q, rows, :]
        for n in range(CHIPS - 1):
            total = total + rsr[q, n]
        pf[q, rows, :] = total
        for n, (dy, dx) in enumerate(offs):
            rcopy(pf.at[q, rows], pf.at[q, rows], s3s.at[q], s3r.at[q], plane(dy, dx, k))
    for q in range(CH):
        wait_for(rsr.at[q], s3r.at[q])
        half = pf.at[q, pl.ds(my_half, HALF)]
        rcopy(half, half, s4s.at[q], s4r.at[q], sib)

    def shard(i):
        return pl.ds(pl.multiple_of(SH * lax.rem(i + 2 * NZ, NZ), 8), SH)

    def ring(q, e):
        if e == 0:
            rcopy(bp.at[q, shard(z + 8)], rr.at[q, 0], ring_s.at[q, 0], rsem_r.at[q, 0], right_dev)
            rcopy(bp.at[q, shard(z - 7)], rl.at[q, 0], ring_s.at[q, 1], rsem_l.at[q, 0], left_dev)
        elif e < 8:
            wait_for(rr.at[q, e - 1], rsem_r.at[q, e - 1])
            rr[q, e - 1] = rr[q, e - 1] + bp[q, shard(z + 8 - e), :]
            rcopy(rr.at[q, e - 1], rr.at[q, e], ring_s.at[q, 0], rsem_r.at[q, e], right_dev)
            wait_for(rl.at[q, e - 1], rsem_l.at[q, e - 1])
            if e < 7:
                rl[q, e - 1] = rl[q, e - 1] + bp[q, shard(z - 7 + e), :]
                rcopy(rl.at[q, e - 1], rl.at[q, e], ring_s.at[q, 1], rsem_l.at[q, e], left_dev)
        elif e == 8:
            wait_for(rr.at[q, 7], rsem_r.at[q, 7])
            own = shard(z)
            bfull[q, own, :] = bp[q, own, :] + rl[q, 6] + rr[q, 7]
            blk = bfull.at[q, own]
            rcopy(blk, blk, ring_s.at[q, 0], asem_r.at[q, 0], right_dev)
            rcopy(blk, blk, ring_s.at[q, 1], asem_l.at[q, 0], left_dev)
        else:
            n = e - 9
            blk = bfull.at[q, shard(z - 1 - n)]
            wait_for(blk, asem_r.at[q, n])
            if e < 16:
                rcopy(blk, blk, ring_s.at[q, 0], asem_r.at[q, n + 1], right_dev)
                blk = bfull.at[q, shard(z + 1 + n)]
                wait_for(blk, asem_l.at[q, n])
                if e < 15:
                    rcopy(blk, blk, ring_s.at[q, 1], asem_l.at[q, n + 1], left_dev)

    for q in range(CH):
        wait_for(sibr.at[q], s4r.at[q])
        high, low = split(pf[q])
        cols = slice(LW * q, LW * q + LW)
        ph[:, cols] = high
        plo[:, cols] = low
        both = jnp.concatenate([high, low], axis=1)
        for r in range(7):
            rows = pl.ds(128 * r, 128)
            part = dot1(mt[rows, :], both, NN)
            bp[q, rows, :] = part[:, :128] + part[:, 128:]
        ring(q, 0)

    owner = jnp.logical_and(z % 3 == 0, z < 15)
    my_u = lax.rem(z // 3, OWN)
    my_tiles = OWN * mine

    def chol():
        for b, (i, j) in enumerate(BLOCKS):
            gl[b * 16 : b * 16 + 16] = doth(pf[i], pf[j], TN).reshape(16, 8, 128)
        for u in range(OWN):
            @pl.when(z != 3 * u)
            def _():
                rcopy(gl.at[my_tiles + u], gr.at[z], gzs, gzr, dev(3 * u, y, x, k))
        yield
        @pl.when(owner)
        def _():
            wait_for(gr.at[pl.ds(0, NZ - 1)], gzr)
            gr[z] = gl[my_tiles + my_u]
            total = gr[0]
            for n in range(1, NZ):
                total = total + gr[n]
            dst = gt.at[my_tiles + my_u]
            gt[my_tiles + my_u] = total
            for dz in range(1, NZ):
                rcopy(dst, dst, gbs, gbr, dev((z + dz) % NZ, y, x, k))
        yield
        own = gt.at[pl.ds(my_tiles, OWN)]
        @pl.when(owner)
        def _():
            wait_for(gt.at[pl.ds(0, OWN - 1)], gbr)
        @pl.when(jnp.logical_not(owner))
        def _():
            wait_for(gt.at[pl.ds(0, OWN)], gbr)
        for n, (dy, dx) in enumerate(offs):
            rcopy(own, own, gps, gpr, plane(dy, dx, k))
        yield
        wait_for(gt.at[pl.ds(0, OWN * (CHIPS - 1))], gpr)
        half = gt.at[pl.ds(OWN * CHIPS * k, OWN * CHIPS)]
        rcopy(half, half, gss, gsr, sib)
        yield
        wait_for(gt.at[pl.ds(0, OWN * CHIPS)], gsr)
        for b, (i, j) in enumerate(BLOCKS):
            g[128 * i : 128 * i + 128, 128 * j : 128 * j + 128] = gt[16 * b : 16 * b + 16].reshape(128, 128)
        yield
        eye = lax.broadcasted_iota(jnp.int32, (128, 128), 0) == lax.broadcasted_iota(jnp.int32, (128, 128), 1)
        for kb in range(4):
            K = slice(128 * kb, 128 * kb + 128)
            before = slice(0, 128 * kb)
            wd[...] = eye.astype(F32)
            for t in range(16):
                leaf(g.at[K, K], wd, t)
                yield
            w = wd[...]
            li[K, K] = w
            if kb:
                li[K, before] = doth(w, li[K, before], NN)
            if kb < 3:
                R = slice(128 * (kb + 1), 512)
                lp = doth(g[R, K], w, NT)
                g[R, R] = g[R, R] - doth(lp, lp, NT)
                yield
                if kb:
                    li[R, before] = li[R, before] - doth(lp, li[K, before], NN)
                li[R, K] = -doth(lp, w, NN)
                li[K, 128 * (kb + 1) :] = jnp.zeros((128, 512 - 128 * (kb + 1)), F32)
            yield
        lh[...], ll[...] = split(li[...])
        yield
        for j in range(4):
            K = 128 * (j + 1)
            J = slice(128 * j, 128 * j + 128)
            a, b = lh[J, :K], ll[J, :K]
            orth = dot1(ph[:, :K], a, NT) + (dot1(ph[:, :K], b, NT) + dot1(plo[:, :K], a, NT))
            oh[:, J] = orth.astype(BF16)
            lf[:, J] = jnp.sqrt(F32(NZ * ROWS_L)) * orth
            yield
        pltpu.make_async_copy(lf, left_out, out_s.at[0]).start()
        yield

    work = chol()
    done = object()

    def pull(n):
        for _ in range(n):
            next(work, done)

    pull(1)
    for e in range(1, 16):
        for q in range(CH):
            ring(q, e)
            if e <= 4:
                if q == CH - 1:
                    pull(1)
            else:
                pull(2)
    while next(work, done) is not done:
        pass

    for q in range(CH):
        ring(q, 16)
        J = slice(128 * q, 128 * q + 128)
        bh[:, J], bl[:, J] = split(bfull[q])
        K = 128 * (q + 1)
        a, b = lh[J, :K], ll[J, :K]
        part = dot1(bh[:, :K], a, NT) + (dot1(bh[:, :K], b, NT) + dot1(bl[:, :K], a, NT))
        back[:, J] = part
        nsq[q : q + 1, :] = jnp.sum(part * part, axis=0, keepdims=True)
    nsq[4:8, :] = jnp.zeros((4, 128), F32)
    rcopy(nsq, nr.at[0], ns, nrs, sib)
    for n, (dy, dx) in enumerate(offs):
        for kk in range(2):
            rcopy(nsq, nr.at[1 + 2 * n + kk], ns, nrs, plane(dy, dx, jnp.where(kk == 0, k, 1 - k)))

    for r in range(4):
        rows = slice(128 * r, 128 * r + 128)
        for cc in range(7):
            cols = slice(128 * cc, 128 * cc + 128)
            update = dot1(oh[rows, :], back[cols, :].astype(BF16), NT)
            mn[rows, cols] = (buf[rows, cols].astype(F32) - F32(1.0 - decay) * update).astype(BF16)
    out_mom = pltpu.make_async_copy(mn, mom_out, out_s.at[1])
    out_mom.start()

    wait_for(nr.at[pl.ds(0, 31)], nrs)
    total = nsq[...]
    for n in range(31):
        total = total + nr[n]
    scale = jnp.sqrt(F32(2 * CHIPS * COLS_L)) * lax.rsqrt(total + 1e-06)
    for q in range(CH):
        J = slice(128 * q, 128 * q + 128)
        back[:, J] = back[:, J] * scale[q : q + 1, :]
    out_right = pltpu.make_async_copy(back, right_out, out_s.at[2])
    out_right.start()

    for q in range(CH):
        wait_for(sibr.at[q], s1s.at[q])
        wait_for(rsr.at[q], s2s.at[q])
        wait_for(rsr.at[q], s3s.at[q])
        wait_for(sibr.at[q], s4s.at[q])
        for _ in range(2):
            wait_for(rr.at[q], ring_s.at[q, 0])
            wait_for(rl.at[q], ring_s.at[q, 1])

    @pl.when(owner)
    def _():
        wait_for(gt.at[pl.ds(0, OWN - 1)], gzs)
        wait_for(gt.at[pl.ds(0, NZ - 1)], gbs)

    @pl.when(jnp.logical_not(owner))
    def _():
        wait_for(gt.at[pl.ds(0, OWN)], gzs)

    wait_for(gt.at[pl.ds(0, OWN * (CHIPS - 1))], gps)
    wait_for(gt.at[pl.ds(0, OWN * CHIPS)], gss)
    wait_for(nr.at[pl.ds(0, 31)], ns)
    pltpu.make_async_copy(lf, left_out, out_s.at[0]).wait()
    out_mom.wait()
    out_right.wait()


def shards(momentum, gradient, basis):
    V = pltpu.VMEM
    D = pltpu.SemaphoreType.DMA
    scratch = [
        V((512, 896), BF16), V((512, 896), BF16), V((896, 512), BF16),
        V((512, 896), BF16), V((896, 512), BF16),
        V((CH, 512, 128), F32), V((CH, HALF, 128), F32), V((CH, CHIPS - 1, PIECE, 128), F32),
        V((CH, 512, 128), F32), V((512, 512), BF16), V((512, 512), BF16), V((CH, 896, 128), F32),
        V((CH, 8, SH, 128), F32), V((CH, 7, SH, 128), F32), V((CH, 896, 128), F32),
        V((896, 512), BF16), V((896, 512), BF16),
        V((TILES, 8, 128), F32), V((NZ, 8, 128), F32), V((TILES, 8, 128), F32),
        V((512, 512), F32), V((512, 512), F32), V((128, 128), F32),
        V((512, 512), BF16), V((512, 512), BF16), V((512, 512), F32), V((512, 512), BF16),
        V((896, 512), F32), V((8, 128), F32), V((31, 8, 128), F32), V((512, 896), BF16),
        D((3,)), D((3,)), D((CH,)), D((CH,)), D((CH,)), D((CH,)), D((CH,)), D((CH,)), D((CH,)), D((CH,)),
        D, D, D, D, D, D, D, D,
        D((CH, 2)), D((CH, 8)), D((CH, 7)), D((CH, 8)), D((CH, 7)), D, D,
    ]
    return pl.pallas_call(
        kernel,
        name="dion",
        out_shape=(
            jax.ShapeDtypeStruct((512, 896), BF16),
            jax.ShapeDtypeStruct((512, 512), F32),
            jax.ShapeDtypeStruct((896, 512), F32),
        ),
        in_specs=[pl.BlockSpec(memory_space=pl.ANY)] * 3,
        out_specs=[pl.BlockSpec(memory_space=pl.ANY)] * 3,
        scratch_shapes=scratch,
        compiler_params=pltpu.CompilerParams(
            collective_id=0, has_side_effects=True, vmem_limit_bytes=50 * 2**20
        ),
    )(momentum, gradient, basis)


def solution(mesh):
    in_specs = (P("row", "col"), P("row", "col"), P("col", None))
    out_specs = (P("row", "col"), P("row", None), P("col", None))
    return jax.shard_map(shards, mesh=mesh, in_specs=in_specs, out_specs=out_specs, check_vma=False)
```

```python
import jax
import jax.numpy as jnp
from jax import lax
from jax.experimental import pallas as pl
from jax.experimental.pallas import tpu as pltpu
from jax.sharding import PartitionSpec as P

F32 = jnp.float32
BF16 = jnp.bfloat16
MESH = pl.DeviceIdType.MESH
decay = 0.9

NZ, NY, NX = 16, 4, 4
CHIPS = NY * NX
ROWS_L, COLS_L, RANK = 512, 896, 512
CH = 4
LW = RANK // CH
SH = COLS_L // NZ
HALF = ROWS_L // 2
PIECE = HALF // CHIPS
BLOCKS = [(i, j) for i in range(4) for j in range(i + 1)]
TILES = 16 * len(BLOCKS)
OWN = TILES // (2 * CHIPS)
PLANS = [
    ((8, 7, 6, 5, 4, 3, 2, 0), (7, 6, 5, 4, 3, 2, 1, 0)),
    ((7, 6, 5, 4, 3, 2, 1, 0), (8, 7, 6, 5, 4, 3, 2, 0)),
    ((8, 7, 6, 5, 4, 3, 2, 0), (7, 6, 5, 4, 3, 2, 1, 0)),
    ((7, 6, 5, 4, 3, 2, 1, 0), (8, 7, 6, 5, 4, 3, 2, 0)),
]
SOLO_AT = 2
GRAM_AT = (8, 14, 21, 24)
PER_GAP = 3
NN = ((1,), (0,))
NT = ((1,), (1,))
TN = ((0,), (0,))


def dot1(a, b, dims):
    return lax.dot_general(a, b, (dims, ((), ())), preferred_element_type=F32)


def doth(a, b, dims):
    return lax.dot_general(a, b, (dims, ((), ())), preferred_element_type=F32, precision=lax.Precision.HIGHEST)


def split(a):
    high = a.astype(BF16)
    return high, (a - high.astype(F32)).astype(BF16)


def splat(a, row, lane):
    return jnp.broadcast_to(a[row : row + 1, lane : lane + 1], (8, 128))


def leaf(a_ref, w_ref, t):
    c0 = 8 * t
    ra = [jnp.broadcast_to(a_ref[c0 + i : c0 + i + 1, :], (8, 128)) for i in range(8)]
    s = {(i, j): jnp.broadcast_to(ra[i][:, c0 + j : c0 + j + 1], (8, 128)) for j in range(8) for i in range(j, 8)}
    rw = [jnp.broadcast_to(w_ref[c0 + i : c0 + i + 1, :], (8, 128)) for i in range(8)]
    low = {}
    r = []
    for k in range(8):
        rk = lax.rsqrt(s[k, k])
        r.append(rk)
        ra[k] = ra[k] * rk
        rw[k] = rw[k] * rk
        for i in range(k + 1, 8):
            low[i, k] = s[i, k] * rk
        for j in range(k + 1, 8):
            for i in range(j, 8):
                s[i, j] = s[i, j] - low[i, k] * low[j, k]
        for i in range(k + 1, 8):
            ra[i] = ra[i] - low[i, k] * ra[k]
            rw[i] = rw[i] - low[i, k] * rw[k]
    sub = lax.broadcasted_iota(jnp.int32, (8, 128), 0)
    wt = rw[0]
    for k in range(1, 8):
        wt = jnp.where(sub == k, rw[k], wt)
    for k in range(7, -1, -1):
        ra[k] = ra[k] * r[k]
        rw[k] = rw[k] * r[k]
        for i in range(k):
            ra[i] = ra[i] - low[k, i] * ra[k]
            rw[i] = rw[i] - low[k, i] * rw[k]
    for i in range(t + 1, 16):
        q = slice(8 * i, 8 * i + 8)
        ai = a_ref[q, :]
        ua = uw = None
        for j in range(8):
            m = jnp.broadcast_to(ai[:, c0 + j : c0 + j + 1], (8, 128))
            ua = m * ra[j] if j == 0 else ua + m * ra[j]
            uw = m * rw[j] if j == 0 else uw + m * rw[j]
        a_ref[q, :] = ai - ua
        w_ref[q, :] = w_ref[q, :] - uw
    w_ref[c0 : c0 + 8, :] = wt


def kernel(
    m_hbm, g_hbm, q_hbm, mn, lf, back,
    mv, gv, qv, buf, mt, pp, sibr, rsr, pf, ph, plo, bp,
    run, solo, bfull, bh, bl, gl, gr, gt, pt, g, li, wd, lh, ll, oh, bb, nsq, nr,
    in_s, s1s, s1r, s2s, s2r, s3s, s3r, s4s, s4r,
    gzs, gzr, gbs, gbr, gps, gpr, gss, gsr,
    ring_s, run_r, solo_r, all_r, skip_r, ns, nrs,
):
    z = lax.axis_index("row")
    c = lax.axis_index("col")
    y, x, k = c // 8, (c // 2) % 4, c % 2
    chip = y * NX + x
    mine = k * CHIPS + chip

    def dev(zz, yy, xx, kk):
        return (zz, (yy * NX + xx) * 2 + kk)

    def plane(dy, dx, kk):
        return dev(z, (y + dy) % NY, (x + dx) % NX, kk)

    def peer_chip(dy, dx):
        return ((y + dy) % NY) * NX + (x + dx) % NX

    offs = [(dy, dx) for dy in range(NY) for dx in range(NX) if dy or dx]
    sib = dev(z, y, x, 1 - k)

    def rcopy(src, dst, ss, rs, device):
        cp = pltpu.make_async_remote_copy(
            src_ref=src, dst_ref=dst, send_sem=ss, recv_sem=rs, device_id=device, device_id_type=MESH
        )
        cp.start()

    finals = []

    def wait_for(ref, sem):
        pltpu.make_async_copy(ref, ref, sem).wait()

    loads = [pltpu.make_async_copy(a, b, in_s.at[i]) for i, (a, b) in enumerate([(m_hbm, mv), (g_hbm, gv), (q_hbm, qv)])]
    for cp in loads:
        cp.start()

    bar = pltpu.get_barrier_semaphore()
    pl.semaphore_signal(bar, inc=1, device_id=sib, device_id_type=MESH)
    for dy, dx in offs:
        for kk in range(2):
            pl.semaphore_signal(bar, inc=1, device_id=plane(dy, dx, kk), device_id_type=MESH)
    for dz in range(1, NZ):
        pl.semaphore_signal(bar, inc=1, device_id=dev((z + dz) % NZ, y, x, k), device_id_type=MESH)

    my_half = pl.multiple_of(HALF * k, HALF)
    other_half = pl.multiple_of(HALF * (1 - k), HALF)
    my_piece = pl.multiple_of(HALF * k + PIECE * chip, PIECE)

    def project(start):
        rows = pl.ds(start, HALF)
        part = dot1(buf[rows, :], qv[...], NN)
        for q in range(CH):
            pp[q, rows, :] = part[:, LW * q : LW * q + LW]

    loads[0].wait()
    loads[1].wait()
    for r in range(4):
        rows = pl.ds(128 * r, 128)
        buf[rows, :] = (mv[rows, :].astype(F32) + gv[rows, :].astype(F32)).astype(BF16)
    loads[2].wait()
    project(other_half)

    pl.semaphore_wait(bar, 31 + NZ - 1)

    for q in range(CH):
        rcopy(pp.at[q, pl.ds(other_half, HALF)], sibr.at[q], s1s.at[q], s1r.at[q], sib)
        finals.append(lambda q=q: wait_for(sibr.at[q], s1s.at[q]))
    project(my_half)
    for q in range(CH):
        wait_for(sibr.at[q], s1r.at[q])
        rows = pl.ds(my_half, HALF)
        pp[q, rows, :] = pp[q, rows, :] + sibr[q]
        for n, (dy, dx) in enumerate(offs):
            piece = pl.multiple_of(HALF * k + PIECE * peer_chip(dy, dx), PIECE)
            rcopy(pp.at[q, pl.ds(piece, PIECE)], rsr.at[q, n], s2s.at[q], s2r.at[q], plane(dy, dx, k))
    for r in range(4):
        mt[:, 128 * r : 128 * r + 128] = buf[128 * r : 128 * r + 128, :].T
    for q in range(CH):
        finals.append(lambda q=q: wait_for(rsr.at[q], s2s.at[q]))
        finals.append(lambda q=q: wait_for(rsr.at[q], s3s.at[q]))
        wait_for(rsr.at[q], s2r.at[q])
        rows = pl.ds(my_piece, PIECE)
        total = pp[q, rows, :]
        for n in range(CHIPS - 1):
            total = total + rsr[q, n]
        pf[q, rows, :] = total
        for n, (dy, dx) in enumerate(offs):
            rcopy(pf.at[q, rows], pf.at[q, rows], s3s.at[q], s3r.at[q], plane(dy, dx, k))
    for q in range(CH):
        wait_for(rsr.at[q], s3r.at[q])
        half = pf.at[q, pl.ds(my_half, HALF)]
        rcopy(half, half, s4s.at[q], s4r.at[q], sib)
        finals.append(lambda q=q: wait_for(sibr.at[q], s4s.at[q]))

    def shard(i):
        return pl.ds(pl.multiple_of(SH * lax.rem(i + 2 * NZ, NZ), 8), SH)

    def zdev(step):
        return dev((z + step + NZ) % NZ, y, x, k)

    def ring_events(q):
        sent = [0, 0]

        def send(src, dst, way, sem, hop):
            sent[way] += 1
            rcopy(src, dst, ring_s.at[q, way], sem, zdev(hop if way == 0 else -hop))

        def at(way, dist):
            return shard(z + dist if way == 0 else z - dist)

        def finish(way):
            def fn():
                for n in range(0, sent[way], NZ):
                    wait_for(bfull.at[q, pl.ds(0, SH * min(NZ, sent[way] - n))], ring_s.at[q, way])
            return fn

        finals.append(finish(0))
        finals.append(finish(1))
        hops = [len(PLANS[q][0]) - 1, len(PLANS[q][1]) - 1]
        for way in range(2):
            stops = PLANS[q][way]
            send(bp.at[q, at(way, stops[0])], run.at[q, way, 0], way, run_r.at[q, way, 0], stops[0] - stops[1])

        def solos():
            for way in range(2):
                stops = PLANS[q][way]
                for i in range(hops[way]):
                    if stops[i] - stops[i + 1] == 2:
                        send(bp.at[q, at(way, stops[i] - 1)], solo.at[q, way, i], way, solo_r.at[q, way, i], 1)

        if SOLO_AT == 0:
            solos()
        yield

        def arrived(way, i):
            stops = PLANS[q][way]
            wait_for(run.at[q, way, i], run_r.at[q, way, i])
            total = run[q, way, i]
            if stops[i] - stops[i + 1] == 2:
                wait_for(solo.at[q, way, i], solo_r.at[q, way, i])
                total = total + solo[q, way, i]
            return total

        for i in range(1, max(hops)):
            for way in range(2):
                stops = PLANS[q][way]
                if i < hops[way]:
                    run[q, way, i - 1] = arrived(way, i - 1) + bp[q, at(way, stops[i]), :]
                    send(run.at[q, way, i - 1], run.at[q, way, i], way, run_r.at[q, way, i], stops[i] - stops[i + 1])
            if i == SOLO_AT:
                solos()
            yield
        own = shard(z)
        total = arrived(0, hops[0] - 1) + arrived(1, hops[1] - 1)
        bfull[q, own, :] = bp[q, own, :] + total

        def forward(way, i):
            stops = PLANS[q][way][::-1]
            blk = bfull.at[q, at(way, -stops[i])]
            if i:
                wait_for(blk, all_r.at[q, way, i - 1])
            if i < hops[way]:
                send(blk, blk, way, all_r.at[q, way, i], stops[i + 1] - stops[i])

        def skips(way, i):
            stops = PLANS[q][way][::-1]
            if 0 <= i < hops[way] and stops[i + 1] - stops[i] == 2:
                blk = bfull.at[q, at(way, -stops[i])]
                send(blk, blk, way, skip_r.at[q, way, i], 1)

        for i in range(max(hops) + 1):
            for way in range(2):
                if i <= hops[way]:
                    forward(way, i)
            for way in range(2):
                skips(way, i - 1)
            if i == max(hops):
                for way in range(2):
                    stops = PLANS[q][way][::-1]
                    for n in range(hops[way]):
                        if stops[n + 1] - stops[n] == 2:
                            wait_for(bfull.at[q, at(way, -stops[n] - 1)], skip_r.at[q, way, n])
            yield

    events = []
    for q in range(CH):
        wait_for(sibr.at[q], s4r.at[q])
        high, low = split(pf[q])
        cols = slice(LW * q, LW * q + LW)
        ph[:, cols] = high
        plo[:, cols] = low
        both = jnp.concatenate([high, low], axis=1)
        for r in range(7):
            rows = pl.ds(128 * r, 128)
            part = dot1(mt[rows, :], both, NN)
            bp[q, rows, :] = part[:, :128] + part[:, 128:]
        events.append(ring_events(q))
        next(events[q])
        pt[cols, :] = pf[q].T

    my_u = (z % 8) * 3 % 8
    owner = my_u < OWN
    my_u = my_u % OWN
    my_tiles = OWN * mine

    def chol():
        for u in range(OWN):
            tile = my_tiles + u
            b = tile // 16
            i = (b + 9) // 10 + (b + 7) // 10 + (b + 4) // 10
            j = b - i * (i + 1) // 2
            lhs = pt[pl.ds(pl.multiple_of(128 * i + 8 * (tile % 16), 8), 8), :]
            gl[u] = doth(lhs, pf[j], NN)
        for u in range(OWN):
            for far in (0, 8):
                at_z = (3 * u + far) % NZ

                @pl.when(z != at_z)
                def _():
                    rcopy(gl.at[u], gr.at[z], gzs, gzr, dev(at_z, y, x, k))

        def f1():
            @pl.when(owner)
            def _():
                wait_for(gt.at[pl.ds(0, 2 * OWN - 1)], gzs)
                wait_for(gt.at[pl.ds(0, 7)], gbs)

            @pl.when(jnp.logical_not(owner))
            def _():
                wait_for(gt.at[pl.ds(0, 2 * OWN)], gzs)

        finals.append(f1)
        finals.append(lambda: wait_for(gt.at[pl.ds(0, OWN * (CHIPS - 1))], gps))
        finals.append(lambda: wait_for(gt.at[pl.ds(0, OWN * CHIPS)], gss))
        yield
        @pl.when(owner)
        def _():
            wait_for(gr.at[pl.ds(0, NZ - 1)], gzr)
            gr[z] = gl[my_u]
            total = gr[0]
            for n in range(1, NZ):
                total = total + gr[n]
            dst = gt.at[my_tiles + my_u]
            gt[my_tiles + my_u] = total
            for dz in (1, -1, 2, -2, 3, -3, 4):
                rcopy(dst, dst, gbs, gbr, dev((z + dz + NZ) % NZ, y, x, k))
        yield
        own = gt.at[pl.ds(my_tiles, OWN)]
        @pl.when(owner)
        def _():
            wait_for(gt.at[pl.ds(0, OWN - 1)], gbr)
        @pl.when(jnp.logical_not(owner))
        def _():
            wait_for(gt.at[pl.ds(0, OWN)], gbr)
        for n, (dy, dx) in enumerate(offs):
            rcopy(own, own, gps, gpr, plane(dy, dx, k))
        yield
        wait_for(gt.at[pl.ds(0, OWN * (CHIPS - 1))], gpr)
        half = gt.at[pl.ds(OWN * CHIPS * k, OWN * CHIPS)]
        rcopy(half, half, gss, gsr, sib)
        yield
        wait_for(gt.at[pl.ds(0, OWN * CHIPS)], gsr)
        for b, (i, j) in enumerate(BLOCKS):
            g[128 * i : 128 * i + 128, 128 * j : 128 * j + 128] = gt[16 * b : 16 * b + 16].reshape(128, 128)
        yield
        eye = lax.broadcasted_iota(jnp.int32, (128, 128), 0) == lax.broadcasted_iota(jnp.int32, (128, 128), 1)
        for kb in range(4):
            K = slice(128 * kb, 128 * kb + 128)
            before = slice(0, 128 * kb)
            wd[...] = eye.astype(F32)
            for t in range(16):
                leaf(g.at[K, K], wd, t)
                yield
            w = wd[...]
            li[K, K] = w
            if kb:
                li[K, before] = doth(w, li[K, before], NN)
            if kb < 3:
                R = slice(128 * (kb + 1), 512)
                lp = doth(g[R, K], w, NT)
                g[R, R] = g[R, R] - doth(lp, lp, NT)
                yield
                if kb:
                    li[R, before] = li[R, before] - doth(lp, li[K, before], NN)
                li[R, K] = -doth(lp, w, NN)
                li[K, 128 * (kb + 1) :] = jnp.zeros((128, 512 - 128 * (kb + 1)), F32)
            yield
        lh[...], ll[...] = split(li[...])
        yield

    work = chol()
    done = object()

    def pull(n):
        for _ in range(n):
            next(work, done)

    pull(1)
    last = max(len(p) - 1 for plan in PLANS for p in plan) * 2
    count = 0
    for e in range(1, last + 1):
        for q in range(CH):
            if next(events[q], done) is done:
                continue
            count += 1
            if count in GRAM_AT:
                pull(1)
            elif count > GRAM_AT[-1]:
                pull(PER_GAP)
    while next(work, done) is not done:
        pass

    for q in range(CH):
        J = slice(128 * q, 128 * q + 128)
        bh[:, J], bl[:, J] = split(bfull[q])
    for h in range(2):
        J = slice(256 * h, 256 * h + 256)
        K = 256 * (h + 1)
        a, b = lh[J, :K], ll[J, :K]
        part = dot1(bh[:, :K], a, NT) + (dot1(bh[:, :K], b, NT) + dot1(bl[:, :K], a, NT))
        back[:, J] = part
        bb[:, J] = part.astype(BF16)
        sq = jnp.sum(part * part, axis=0, keepdims=True)
        nsq[2 * h : 2 * h + 1, :] = sq[:, :128]
        nsq[2 * h + 1 : 2 * h + 2, :] = sq[:, 128:]
    nsq[4:8, :] = jnp.zeros((4, 128), F32)
    rcopy(nsq, nr.at[0], ns, nrs, sib)
    for n, (dy, dx) in enumerate(offs):
        for kk in range(2):
            rcopy(nsq, nr.at[1 + 2 * n + kk], ns, nrs, plane(dy, dx, jnp.where(kk == 0, k, 1 - k)))

    for h in range(2):
        J = slice(256 * h, 256 * h + 256)
        K = 256 * (h + 1)
        a, b = lh[J, :K], ll[J, :K]
        orth = dot1(ph[:, :K], a, NT) + (dot1(ph[:, :K], b, NT) + dot1(plo[:, :K], a, NT))
        oh[:, J] = orth.astype(BF16)
        lf[:, J] = jnp.sqrt(F32(NZ * ROWS_L)) * orth
    for first in range(0, COLS_L, 256):
        cols = slice(first, min(first + 256, COLS_L))
        update = dot1(oh[...], bb[cols, :], NT)
        mn[:, cols] = (buf[:, cols].astype(F32) - F32(1.0 - decay) * update).astype(BF16)

    wait_for(nr.at[pl.ds(0, 31)], nrs)
    total = nsq[...]
    for n in range(31):
        total = total + nr[n]
    scale = jnp.sqrt(F32(2 * CHIPS * COLS_L)) * lax.rsqrt(total + 1e-06)
    for q in range(CH):
        J = slice(128 * q, 128 * q + 128)
        back[:, J] = back[:, J] * scale[q : q + 1, :]

    wait_for(nr.at[pl.ds(0, 31)], ns)
    for fn in finals:
        fn()


def finish(mom, left, right, mom_out, left_out, right_out, sems):
    pairs = [(right, right_out), (left, left_out), (mom, mom_out)]
    copies = [pltpu.make_async_copy(a, b, sems.at[n]) for n, (a, b) in enumerate(pairs)]
    for cp in copies:
        cp.start()
    for cp in copies:
        cp.wait()


def shards(momentum, gradient, basis):
    V = pltpu.VMEM
    D = pltpu.SemaphoreType.DMA
    scratch = [
        V((512, 896), BF16), V((512, 896), BF16), V((896, 512), BF16),
        V((512, 896), BF16), V((896, 512), BF16),
        V((CH, 512, 128), F32), V((CH, HALF, 128), F32), V((CH, CHIPS - 1, PIECE, 128), F32),
        V((CH, 512, 128), F32), V((512, 512), BF16), V((512, 512), BF16), V((CH, 896, 128), F32),
        V((CH, 2, 8, SH, 128), F32), V((CH, 2, 8, SH, 128), F32), V((CH, 896, 128), F32),
        V((896, 512), BF16), V((896, 512), BF16),
        V((OWN, 8, 128), F32), V((NZ, 8, 128), F32), V((TILES, 8, 128), F32),
        V((512, 512), F32), V((512, 512), F32), V((512, 512), F32), V((128, 128), F32),
        V((512, 512), BF16), V((512, 512), BF16), V((512, 512), BF16),
        V((896, 512), BF16), V((8, 128), F32), V((31, 8, 128), F32),
        D((3,)), D((CH,)), D((CH,)), D((CH,)), D((CH,)), D((CH,)), D((CH,)), D((CH,)), D((CH,)),
        D, D, D, D, D, D, D, D,
        D((CH, 2)), D((CH, 2, 8)), D((CH, 2, 8)), D((CH, 2, 8)), D((CH, 2, 8)), D, D,
    ]
    results = pl.pallas_call(
        kernel,
        name="dion",
        out_shape=(
            pltpu.VMEM((512, 896), BF16),
            pltpu.VMEM((512, 512), F32),
            pltpu.VMEM((896, 512), F32),
        ),
        in_specs=[pl.BlockSpec(memory_space=pltpu.HBM)] * 3,
        out_specs=[pl.BlockSpec(memory_space=pltpu.VMEM)] * 3,
        scratch_shapes=scratch,
        compiler_params=pltpu.CompilerParams(
            collective_id=0, has_side_effects=True, vmem_limit_bytes=40 * 2**20
        ),
    )(*[pltpu.with_memory_space_constraint(a, pltpu.HBM) for a in (momentum, gradient, basis)])
    return pl.pallas_call(
        finish,
        name="finish",
        out_shape=(
            jax.ShapeDtypeStruct((512, 896), BF16),
            jax.ShapeDtypeStruct((512, 512), F32),
            jax.ShapeDtypeStruct((896, 512), F32),
        ),
        in_specs=[pl.BlockSpec(memory_space=pl.ANY)] * 3,
        out_specs=[pl.BlockSpec(memory_space=pl.ANY)] * 3,
        scratch_shapes=[D((3,))],
        compiler_params=pltpu.CompilerParams(vmem_limit_bytes=4 * 2**20),
    )(*results)


def solution(mesh):
    in_specs = (P("row", "col"), P("row", "col"), P("col", None))
    out_specs = (P("row", "col"), P("row", None), P("col", None))
    return jax.shard_map(shards, mesh=mesh, in_specs=in_specs, out_specs=out_specs, check_vma=False)
```

```python
import jax
import jax.numpy as jnp
from jax import lax
from jax.experimental import pallas as pl
from jax.experimental.pallas import tpu as pltpu
from jax.sharding import PartitionSpec as P

F32 = jnp.float32
BF16 = jnp.bfloat16
MESH = pl.DeviceIdType.MESH
decay = 0.9

NZ, NY, NX = 16, 4, 4
CHIPS = NY * NX
ROWS_L, COLS_L, RANK = 512, 896, 512
CH = 4
LW = RANK // CH
SH = COLS_L // NZ
HALF = ROWS_L // 2
PIECE = HALF // CHIPS
BLOCKS = [(i, j) for i in range(4) for j in range(i + 1)]
TILES = 16 * len(BLOCKS)
OWN = TILES // (2 * CHIPS)
PLANS = [
    ((8, 7, 6, 5, 4, 3, 2, 0), (7, 6, 5, 4, 3, 2, 1, 0)),
    ((7, 6, 5, 4, 3, 2, 1, 0), (8, 7, 6, 5, 4, 3, 2, 0)),
    ((8, 7, 6, 5, 4, 3, 2, 0), (7, 6, 5, 4, 3, 2, 1, 0)),
    ((7, 6, 5, 4, 3, 2, 1, 0), (8, 7, 6, 5, 4, 3, 2, 0)),
]
SOLO_AT = 2
NORM_GAPS = 6
HEAD_AT = (3, 9)
GRAM_AT = (8, 14, 21, 24)
PER_GAP = 3
NN = ((1,), (0,))
NT = ((1,), (1,))
TN = ((0,), (0,))


def dot1(a, b, dims):
    return lax.dot_general(a, b, (dims, ((), ())), preferred_element_type=F32)


def doth(a, b, dims):
    return lax.dot_general(a, b, (dims, ((), ())), preferred_element_type=F32, precision=lax.Precision.HIGHEST)


def split(a):
    high = a.astype(BF16)
    return high, (a - high.astype(F32)).astype(BF16)


def splat(a, row, lane):
    return jnp.broadcast_to(a[row : row + 1, lane : lane + 1], (8, 128))


def leaf(a_ref, w_ref, t):
    c0 = 8 * t
    ra = [jnp.broadcast_to(a_ref[c0 + i : c0 + i + 1, :], (8, 128)) for i in range(8)]
    s = {(i, j): jnp.broadcast_to(ra[i][:, c0 + j : c0 + j + 1], (8, 128)) for j in range(8) for i in range(j, 8)}
    rw = [jnp.broadcast_to(w_ref[c0 + i : c0 + i + 1, :], (8, 128)) for i in range(8)]
    low = {}
    r = []
    for k in range(8):
        rk = lax.rsqrt(s[k, k])
        r.append(rk)
        ra[k] = ra[k] * rk
        rw[k] = rw[k] * rk
        for i in range(k + 1, 8):
            low[i, k] = s[i, k] * rk
        for j in range(k + 1, 8):
            for i in range(j, 8):
                s[i, j] = s[i, j] - low[i, k] * low[j, k]
        for i in range(k + 1, 8):
            ra[i] = ra[i] - low[i, k] * ra[k]
            rw[i] = rw[i] - low[i, k] * rw[k]
    sub = lax.broadcasted_iota(jnp.int32, (8, 128), 0)
    wt = rw[0]
    for k in range(1, 8):
        wt = jnp.where(sub == k, rw[k], wt)
    for k in range(7, -1, -1):
        ra[k] = ra[k] * r[k]
        rw[k] = rw[k] * r[k]
        for i in range(k):
            ra[i] = ra[i] - low[k, i] * ra[k]
            rw[i] = rw[i] - low[k, i] * rw[k]
    for i in range(t + 1, 16):
        q = slice(8 * i, 8 * i + 8)
        ai = a_ref[q, :]
        ua = uw = None
        for j in range(8):
            m = jnp.broadcast_to(ai[:, c0 + j : c0 + j + 1], (8, 128))
            ua = m * ra[j] if j == 0 else ua + m * ra[j]
            uw = m * rw[j] if j == 0 else uw + m * rw[j]
        a_ref[q, :] = ai - ua
        w_ref[q, :] = w_ref[q, :] - uw
    w_ref[c0 : c0 + 8, :] = wt


def kernel(
    m_hbm, g_hbm, q_hbm, mn, lf, back,
    mv, gv, qv, buf, mt, pp, sibr, rsr, pf, ph, plo, bp,
    run, solo, bfull, bh, bl, gl, gr, gt, ha, hp, ht, pt, g, li, wd, lh, ll, oh, bb, nsq, nr, nt, nz,
    in_s, s1s, s1r, s2s, s2r, s3s, s3r, s4s, s4r,
    gzs, gzr, gbs, gbr, gps, gpr, gss, gsr, has, har, hbs, hbr, nzs, nzr,
    ring_s, run_r, solo_r, all_r, skip_r, ns, nrs,
):
    z = lax.axis_index("row")
    c = lax.axis_index("col")
    y, x, k = c // 8, (c // 2) % 4, c % 2
    chip = y * NX + x
    mine = k * CHIPS + chip

    def dev(zz, yy, xx, kk):
        return (zz, (yy * NX + xx) * 2 + kk)

    def plane(dy, dx, kk):
        return dev(z, (y + dy) % NY, (x + dx) % NX, kk)

    def peer_chip(dy, dx):
        return ((y + dy) % NY) * NX + (x + dx) % NX

    offs = [(dy, dx) for dy in range(NY) for dx in range(NX) if dy or dx]
    sib = dev(z, y, x, 1 - k)

    def rcopy(src, dst, ss, rs, device):
        cp = pltpu.make_async_remote_copy(
            src_ref=src, dst_ref=dst, send_sem=ss, recv_sem=rs, device_id=device, device_id_type=MESH
        )
        cp.start()

    finals = []

    def wait_for(ref, sem):
        pltpu.make_async_copy(ref, ref, sem).wait()

    loads = [pltpu.make_async_copy(a, b, in_s.at[i]) for i, (a, b) in enumerate([(m_hbm, mv), (g_hbm, gv), (q_hbm, qv)])]
    for cp in loads:
        cp.start()

    bar = pltpu.get_barrier_semaphore()
    pl.semaphore_signal(bar, inc=1, device_id=sib, device_id_type=MESH)
    for dy, dx in offs:
        for kk in range(2):
            pl.semaphore_signal(bar, inc=1, device_id=plane(dy, dx, kk), device_id_type=MESH)
    for dz in range(1, NZ):
        pl.semaphore_signal(bar, inc=1, device_id=dev((z + dz) % NZ, y, x, k), device_id_type=MESH)

    my_half = pl.multiple_of(HALF * k, HALF)
    other_half = pl.multiple_of(HALF * (1 - k), HALF)
    my_piece = pl.multiple_of(HALF * k + PIECE * chip, PIECE)

    def project(start):
        rows = pl.ds(start, HALF)
        part = dot1(buf[rows, :], qv[...], NN)
        for q in range(CH):
            pp[q, rows, :] = part[:, LW * q : LW * q + LW]

    loads[0].wait()
    loads[1].wait()
    for r in range(4):
        rows = pl.ds(128 * r, 128)
        buf[rows, :] = (mv[rows, :].astype(F32) + gv[rows, :].astype(F32)).astype(BF16)
    loads[2].wait()
    project(other_half)

    pl.semaphore_wait(bar, 31 + NZ - 1)

    for q in range(CH):
        rcopy(pp.at[q, pl.ds(other_half, HALF)], sibr.at[q], s1s.at[q], s1r.at[q], sib)
        finals.append(lambda q=q: wait_for(sibr.at[q], s1s.at[q]))
    project(my_half)
    for q in range(CH):
        wait_for(sibr.at[q], s1r.at[q])
        rows = pl.ds(my_half, HALF)
        pp[q, rows, :] = pp[q, rows, :] + sibr[q]
        for n, (dy, dx) in enumerate(offs):
            piece = pl.multiple_of(HALF * k + PIECE * peer_chip(dy, dx), PIECE)
            rcopy(pp.at[q, pl.ds(piece, PIECE)], rsr.at[q, n], s2s.at[q], s2r.at[q], plane(dy, dx, k))
    for r in range(4):
        mt[:, 128 * r : 128 * r + 128] = buf[128 * r : 128 * r + 128, :].T
    for q in range(CH):
        finals.append(lambda q=q: wait_for(rsr.at[q], s2s.at[q]))
        finals.append(lambda q=q: wait_for(rsr.at[q], s3s.at[q]))
        wait_for(rsr.at[q], s2r.at[q])
        rows = pl.ds(my_piece, PIECE)
        total = pp[q, rows, :]
        for n in range(CHIPS - 1):
            total = total + rsr[q, n]
        pf[q, rows, :] = total
        for n, (dy, dx) in enumerate(offs):
            rcopy(pf.at[q, rows], pf.at[q, rows], s3s.at[q], s3r.at[q], plane(dy, dx, k))
    for q in range(CH):
        wait_for(rsr.at[q], s3r.at[q])
        half = pf.at[q, pl.ds(my_half, HALF)]
        rcopy(half, half, s4s.at[q], s4r.at[q], sib)
        finals.append(lambda q=q: wait_for(sibr.at[q], s4s.at[q]))

    def shard(i):
        return pl.ds(pl.multiple_of(SH * lax.rem(i + 2 * NZ, NZ), 8), SH)

    def zdev(step):
        return dev((z + step + NZ) % NZ, y, x, k)

    def ring_events(q):
        sent = [0, 0]

        def send(src, dst, way, sem, hop):
            sent[way] += 1
            rcopy(src, dst, ring_s.at[q, way], sem, zdev(hop if way == 0 else -hop))

        def at(way, dist):
            return shard(z + dist if way == 0 else z - dist)

        def finish(way):
            def fn():
                for n in range(0, sent[way], NZ):
                    wait_for(bfull.at[q, pl.ds(0, SH * min(NZ, sent[way] - n))], ring_s.at[q, way])
            return fn

        finals.append(finish(0))
        finals.append(finish(1))
        hops = [len(PLANS[q][0]) - 1, len(PLANS[q][1]) - 1]
        for way in range(2):
            stops = PLANS[q][way]
            send(bp.at[q, at(way, stops[0])], run.at[q, way, 0], way, run_r.at[q, way, 0], stops[0] - stops[1])

        def solos():
            for way in range(2):
                stops = PLANS[q][way]
                for i in range(hops[way]):
                    if stops[i] - stops[i + 1] == 2:
                        send(bp.at[q, at(way, stops[i] - 1)], solo.at[q, way, i], way, solo_r.at[q, way, i], 1)

        if SOLO_AT == 0:
            solos()
        yield

        def arrived(way, i):
            stops = PLANS[q][way]
            wait_for(run.at[q, way, i], run_r.at[q, way, i])
            total = run[q, way, i]
            if stops[i] - stops[i + 1] == 2:
                wait_for(solo.at[q, way, i], solo_r.at[q, way, i])
                total = total + solo[q, way, i]
            return total

        for i in range(1, max(hops)):
            for way in range(2):
                stops = PLANS[q][way]
                if i < hops[way]:
                    run[q, way, i - 1] = arrived(way, i - 1) + bp[q, at(way, stops[i]), :]
                    send(run.at[q, way, i - 1], run.at[q, way, i], way, run_r.at[q, way, i], stops[i] - stops[i + 1])
            if i == SOLO_AT:
                solos()
            yield
        own = shard(z)
        total = arrived(0, hops[0] - 1) + arrived(1, hops[1] - 1)
        bfull[q, own, :] = bp[q, own, :] + total

        def forward(way, i):
            stops = PLANS[q][way][::-1]
            blk = bfull.at[q, at(way, -stops[i])]
            if i:
                wait_for(blk, all_r.at[q, way, i - 1])
            if i < hops[way]:
                send(blk, blk, way, all_r.at[q, way, i], stops[i + 1] - stops[i])

        def skips(way, i):
            stops = PLANS[q][way][::-1]
            if 0 <= i < hops[way] and stops[i + 1] - stops[i] == 2:
                blk = bfull.at[q, at(way, -stops[i])]
                send(blk, blk, way, skip_r.at[q, way, i], 1)

        for i in range(max(hops) + 1):
            for way in range(2):
                if i <= hops[way]:
                    forward(way, i)
            for way in range(2):
                skips(way, i - 1)
            if i == max(hops):
                for way in range(2):
                    stops = PLANS[q][way][::-1]
                    for n in range(hops[way]):
                        if stops[n + 1] - stops[n] == 2:
                            wait_for(bfull.at[q, at(way, -stops[n] - 1)], skip_r.at[q, way, n])
            yield

    events = []
    for q in range(CH):
        wait_for(sibr.at[q], s4r.at[q])
        high, low = split(pf[q])
        cols = slice(LW * q, LW * q + LW)
        ph[:, cols] = high
        plo[:, cols] = low
        both = jnp.concatenate([high, low], axis=1)
        for r in range(7):
            rows = pl.ds(128 * r, 128)
            part = dot1(mt[rows, :], both, NN)
            bp[q, rows, :] = part[:, :128] + part[:, 128:]
        events.append(ring_events(q))
        next(events[q])
        pt[cols, :] = pf[q].T
        if q == 0:
            @pl.when(k == 0)
            def _():
                ha[...] = doth(pt[pl.ds(pl.multiple_of(8 * chip, 8), 8), :], pf[0], NN)
                for dz in range(1, NZ):
                    rcopy(ha, hp.at[z], has, har, dev((z + dz) % NZ, y, x, k))

    my_u = (z % 8) * 3 % 8
    owner = my_u < OWN
    my_u = my_u % OWN
    my_tiles = OWN * mine

    eye = lax.broadcasted_iota(jnp.int32, (128, 128), 0) == lax.broadcasted_iota(jnp.int32, (128, 128), 1)

    def head():
        @pl.when(k == 0)
        def _():
            wait_for(hp.at[pl.ds(0, NZ - 1)], har)
            hp[z] = ha[...]
            total = hp[0]
            for n in range(1, NZ):
                total = total + hp[n]
            ht[chip] = total
            tile = ht.at[chip]
            rcopy(tile, tile, hbs, hbr, sib)
            for dy, dx in offs:
                for kk in range(2):
                    rcopy(tile, tile, hbs, hbr, plane(dy, dx, kk))

        def done_sending():
            @pl.when(k == 0)
            def _():
                wait_for(gt.at[pl.ds(0, NZ - 1)], has)
                wait_for(gt.at[pl.ds(0, 31)], hbs)

        finals.append(done_sending)
        yield

        @pl.when(k == 0)
        def _():
            wait_for(gt.at[pl.ds(0, CHIPS - 1)], hbr)

        @pl.when(k == 1)
        def _():
            wait_for(gt.at[pl.ds(0, CHIPS)], hbr)

        g[:128, :128] = ht[...].reshape(128, 128)
        wd[...] = eye.astype(F32)
        yield
        for t in range(16):
            leaf(g.at[:128, :128], wd, t)
            yield

    def chol():
        for u in range(OWN):
            tile = my_tiles + u
            b = tile // 16
            i = (b + 9) // 10 + (b + 7) // 10 + (b + 4) // 10
            j = b - i * (i + 1) // 2
            lhs = pt[pl.ds(pl.multiple_of(128 * i + 8 * (tile % 16), 8), 8), :]
            gl[u] = doth(lhs, pf[j], NN)
        for u in range(OWN):
            for far in (0, 8):
                at_z = (3 * u + far) % NZ

                @pl.when(z != at_z)
                def _():
                    rcopy(gl.at[u], gr.at[z], gzs, gzr, dev(at_z, y, x, k))

        def f1():
            @pl.when(owner)
            def _():
                wait_for(gt.at[pl.ds(0, 2 * OWN - 1)], gzs)
                wait_for(gt.at[pl.ds(0, 7)], gbs)

            @pl.when(jnp.logical_not(owner))
            def _():
                wait_for(gt.at[pl.ds(0, 2 * OWN)], gzs)

        finals.append(f1)
        finals.append(lambda: wait_for(gt.at[pl.ds(0, OWN * (CHIPS - 1))], gps))
        finals.append(lambda: wait_for(gt.at[pl.ds(0, OWN * CHIPS)], gss))
        yield
        @pl.when(owner)
        def _():
            wait_for(gr.at[pl.ds(0, NZ - 1)], gzr)
            gr[z] = gl[my_u]
            total = gr[0]
            for n in range(1, NZ):
                total = total + gr[n]
            dst = gt.at[my_tiles + my_u]
            gt[my_tiles + my_u] = total
            for dz in (1, -1, 2, -2, 3, -3, 4):
                rcopy(dst, dst, gbs, gbr, dev((z + dz + NZ) % NZ, y, x, k))
        yield
        own = gt.at[pl.ds(my_tiles, OWN)]
        @pl.when(owner)
        def _():
            wait_for(gt.at[pl.ds(0, OWN - 1)], gbr)
        @pl.when(jnp.logical_not(owner))
        def _():
            wait_for(gt.at[pl.ds(0, OWN)], gbr)
        for n, (dy, dx) in enumerate(offs):
            rcopy(own, own, gps, gpr, plane(dy, dx, k))
        yield
        wait_for(gt.at[pl.ds(0, OWN * (CHIPS - 1))], gpr)
        half = gt.at[pl.ds(OWN * CHIPS * k, OWN * CHIPS)]
        rcopy(half, half, gss, gsr, sib)
        yield
        wait_for(gt.at[pl.ds(0, OWN * CHIPS)], gsr)
        for b, (i, j) in enumerate(BLOCKS[1:], 1):
            g[128 * i : 128 * i + 128, 128 * j : 128 * j + 128] = gt[16 * b : 16 * b + 16].reshape(128, 128)
        yield
        yield from first
        for kb in range(4):
            K = slice(128 * kb, 128 * kb + 128)
            before = slice(0, 128 * kb)
            if kb:
                wd[...] = eye.astype(F32)
                for t in range(16):
                    leaf(g.at[K, K], wd, t)
                    yield
            w = wd[...]
            li[K, K] = w
            if kb:
                li[K, before] = doth(w, li[K, before], NN)
            if kb < 3:
                R = slice(128 * (kb + 1), 512)
                lp = doth(g[R, K], w, NT)
                g[R, R] = g[R, R] - doth(lp, lp, NT)
                yield
                if kb:
                    li[R, before] = li[R, before] - doth(lp, li[K, before], NN)
                li[R, K] = -doth(lp, w, NN)
                li[K, 128 * (kb + 1) :] = jnp.zeros((128, 512 - 128 * (kb + 1)), F32)
            yield
        lh[...], ll[...] = split(li[...])
        own = pl.ds(pl.multiple_of(SH * z, 8), SH)
        high, low = split(jnp.concatenate([bfull[q, own, :] for q in range(CH)], axis=1))
        part = dot1(high, lh[...], NT) + (dot1(high, ll[...], NT) + dot1(low, lh[...], NT))
        sq = jnp.sum(part * part, axis=0, keepdims=True)
        for q in range(CH):
            nsq[q : q + 1, :] = sq[:, 128 * q : 128 * q + 128]
        finals.append(lambda: wait_for(nr, ns))
        rcopy(nsq, nr.at[0], ns, nrs, sib)
        for n, (dy, dx) in enumerate(offs):
            for kk in range(2):
                rcopy(nsq, nr.at[1 + 2 * n + kk], ns, nrs, plane(dy, dx, jnp.where(kk == 0, k, 1 - k)))
        yield
        for h in range(2):
            J = slice(256 * h, 256 * h + 256)
            K = 256 * (h + 1)
            a, b = lh[J, :K], ll[J, :K]
            orth = dot1(ph[:, :K], a, NT) + (dot1(ph[:, :K], b, NT) + dot1(plo[:, :K], a, NT))
            oh[:, J] = orth.astype(BF16)
            lf[:, J] = jnp.sqrt(F32(NZ * ROWS_L)) * orth
            yield
        for _ in range(PER_GAP * NORM_GAPS - 2):
            yield
        wait_for(nr, nrs)
        total = nsq[...]
        for n in range(31):
            total = total + nr[n]
        nt[...] = total
        finals.append(lambda: wait_for(nz.at[pl.ds(0, NZ - 1)], nzs))
        for dz in range(1, NZ):
            rcopy(nt, nz.at[z], nzs, nzr, dev((z + dz) % NZ, y, x, k))
        yield

    first = head()
    work = chol()
    done = object()

    def pull(n):
        for _ in range(n):
            next(work, done)

    pull(1)
    last = max(len(p) - 1 for plan in PLANS for p in plan) * 2
    count = 0
    for e in range(1, last + 1):
        for q in range(CH):
            if next(events[q], done) is done:
                continue
            count += 1
            if count in GRAM_AT:
                pull(1)
            elif count > GRAM_AT[-1]:
                pull(PER_GAP)
            if count in HEAD_AT or HEAD_AT[-1] < count < GRAM_AT[-1]:
                next(first, done)
    while next(work, done) is not done:
        pass

    for q in range(CH):
        J = slice(128 * q, 128 * q + 128)
        bh[:, J], bl[:, J] = split(bfull[q])
    for h in range(2):
        J = slice(256 * h, 256 * h + 256)
        K = 256 * (h + 1)
        a, b = lh[J, :K], ll[J, :K]
        part = dot1(bh[:, :K], a, NT) + (dot1(bh[:, :K], b, NT) + dot1(bl[:, :K], a, NT))
        back[:, J] = part
        bb[:, J] = part.astype(BF16)
    for first in range(0, COLS_L, 256):
        cols = slice(first, min(first + 256, COLS_L))
        update = dot1(oh[...], bb[cols, :], NT)
        mn[:, cols] = (buf[:, cols].astype(F32) - F32(1.0 - decay) * update).astype(BF16)

    wait_for(nz.at[pl.ds(0, NZ - 1)], nzr)
    nz[z] = nt[...]
    total = nz[0]
    for n in range(1, NZ):
        total = total + nz[n]
    scale = jnp.sqrt(F32(2 * CHIPS * COLS_L)) * lax.rsqrt(total + 1e-06)
    for q in range(CH):
        J = slice(128 * q, 128 * q + 128)
        back[:, J] = back[:, J] * scale[q : q + 1, :]

    for fn in finals:
        fn()


def finish(mom, left, right, mom_out, left_out, right_out, sems):
    pairs = [(right, right_out), (left, left_out), (mom, mom_out)]
    copies = [pltpu.make_async_copy(a, b, sems.at[n]) for n, (a, b) in enumerate(pairs)]
    for cp in copies:
        cp.start()
    for cp in copies:
        cp.wait()


def shards(momentum, gradient, basis):
    V = pltpu.VMEM
    D = pltpu.SemaphoreType.DMA
    scratch = [
        V((512, 896), BF16), V((512, 896), BF16), V((896, 512), BF16),
        V((512, 896), BF16), V((896, 512), BF16),
        V((CH, 512, 128), F32), V((CH, HALF, 128), F32), V((CH, CHIPS - 1, PIECE, 128), F32),
        V((CH, 512, 128), F32), V((512, 512), BF16), V((512, 512), BF16), V((CH, 896, 128), F32),
        V((CH, 2, 8, SH, 128), F32), V((CH, 2, 8, SH, 128), F32), V((CH, 896, 128), F32),
        V((896, 512), BF16), V((896, 512), BF16),
        V((OWN, 8, 128), F32), V((NZ, 8, 128), F32), V((TILES, 8, 128), F32),
        V((8, 128), F32), V((NZ, 8, 128), F32), V((16, 8, 128), F32),
        V((512, 512), F32), V((512, 512), F32), V((512, 512), F32), V((128, 128), F32),
        V((512, 512), BF16), V((512, 512), BF16), V((512, 512), BF16),
        V((896, 512), BF16), V((4, 128), F32), V((31, 4, 128), F32), V((4, 128), F32), V((NZ, 4, 128), F32),
        D((3,)), D((CH,)), D((CH,)), D((CH,)), D((CH,)), D((CH,)), D((CH,)), D((CH,)), D((CH,)),
        D, D, D, D, D, D, D, D, D, D, D, D, D, D,
        D((CH, 2)), D((CH, 2, 8)), D((CH, 2, 8)), D((CH, 2, 8)), D((CH, 2, 8)), D, D,
    ]
    results = pl.pallas_call(
        kernel,
        name="dion",
        out_shape=(
            pltpu.VMEM((512, 896), BF16),
            pltpu.VMEM((512, 512), F32),
            pltpu.VMEM((896, 512), F32),
        ),
        in_specs=[pl.BlockSpec(memory_space=pltpu.HBM)] * 3,
        out_specs=[pl.BlockSpec(memory_space=pltpu.VMEM)] * 3,
        scratch_shapes=scratch,
        compiler_params=pltpu.CompilerParams(
            collective_id=0, has_side_effects=True, vmem_limit_bytes=40 * 2**20
        ),
    )(*[pltpu.with_memory_space_constraint(a, pltpu.HBM) for a in (momentum, gradient, basis)])
    return pl.pallas_call(
        finish,
        name="finish",
        out_shape=(
            jax.ShapeDtypeStruct((512, 896), BF16),
            jax.ShapeDtypeStruct((512, 512), F32),
            jax.ShapeDtypeStruct((896, 512), F32),
        ),
        in_specs=[pl.BlockSpec(memory_space=pl.ANY)] * 3,
        out_specs=[pl.BlockSpec(memory_space=pl.ANY)] * 3,
        scratch_shapes=[D((3,))],
        compiler_params=pltpu.CompilerParams(vmem_limit_bytes=4 * 2**20),
    )(*results)


def solution(mesh):
    in_specs = (P("row", "col"), P("row", "col"), P("col", None))
    out_specs = (P("row", "col"), P("row", None), P("col", None))
    return jax.shard_map(shards, mesh=mesh, in_specs=in_specs, out_specs=out_specs, check_vma=False)
```

```python
import jax
import jax.numpy as jnp
from jax import lax
from jax.experimental import pallas as pl
from jax.experimental.pallas import tpu as pltpu
from jax.sharding import PartitionSpec as P

F32 = jnp.float32
BF16 = jnp.bfloat16
MESH = pl.DeviceIdType.MESH
decay = 0.9

NZ, NY, NX = 16, 4, 4
CHIPS = NY * NX
ROWS_L, COLS_L, RANK = 512, 896, 512
CH = 4
LW = RANK // CH
SH = COLS_L // NZ
HALF = ROWS_L // 2
PIECE = HALF // CHIPS
BLOCKS = [(i, j) for i in range(4) for j in range(i + 1)]
TILES = 16 * len(BLOCKS)
OWN = TILES // (2 * CHIPS)
PLANS = [
    ((8, 7, 6, 5, 4, 3, 2, 0), (7, 6, 5, 4, 3, 2, 1, 0)),
    ((7, 6, 5, 4, 3, 2, 1, 0), (8, 7, 6, 5, 4, 3, 2, 0)),
    ((8, 7, 6, 5, 4, 3, 2, 0), (7, 6, 5, 4, 3, 2, 1, 0)),
    ((7, 6, 5, 4, 3, 2, 1, 0), (8, 7, 6, 5, 4, 3, 2, 0)),
]
NORM_GAPS = 6
HEAD_AT = (3, 9)
GRAM_AT = (8, 14, 21, 24)
PER_GAP = 3
NN = ((1,), (0,))
NT = ((1,), (1,))
TN = ((0,), (0,))


def dot1(a, b, dims):
    return lax.dot_general(a, b, (dims, ((), ())), preferred_element_type=F32)


def doth(a, b, dims):
    return lax.dot_general(a, b, (dims, ((), ())), preferred_element_type=F32, precision=lax.Precision.HIGHEST)


def split(a):
    high = a.astype(BF16)
    return high, (a - high.astype(F32)).astype(BF16)


def splat(a, row, lane):
    return jnp.broadcast_to(a[row : row + 1, lane : lane + 1], (8, 128))


def leaf(a_ref, w_ref, t):
    c0 = 8 * t
    ra = [jnp.broadcast_to(a_ref[c0 + i : c0 + i + 1, :], (8, 128)) for i in range(8)]
    s = {(i, j): jnp.broadcast_to(ra[i][:, c0 + j : c0 + j + 1], (8, 128)) for j in range(8) for i in range(j, 8)}
    rw = [jnp.broadcast_to(w_ref[c0 + i : c0 + i + 1, :], (8, 128)) for i in range(8)]
    low = {}
    r = []
    for k in range(8):
        rk = lax.rsqrt(s[k, k])
        r.append(rk)
        ra[k] = ra[k] * rk
        rw[k] = rw[k] * rk
        for i in range(k + 1, 8):
            low[i, k] = s[i, k] * rk
        for j in range(k + 1, 8):
            for i in range(j, 8):
                s[i, j] = s[i, j] - low[i, k] * low[j, k]
        for i in range(k + 1, 8):
            ra[i] = ra[i] - low[i, k] * ra[k]
            rw[i] = rw[i] - low[i, k] * rw[k]
    sub = lax.broadcasted_iota(jnp.int32, (8, 128), 0)
    wt = rw[0]
    for k in range(1, 8):
        wt = jnp.where(sub == k, rw[k], wt)
    for k in range(7, -1, -1):
        ra[k] = ra[k] * r[k]
        rw[k] = rw[k] * r[k]
        for i in range(k):
            ra[i] = ra[i] - low[k, i] * ra[k]
            rw[i] = rw[i] - low[k, i] * rw[k]
    for i in range(t + 1, 16):
        q = slice(8 * i, 8 * i + 8)
        ai = a_ref[q, :]
        ua = uw = None
        for j in range(8):
            m = jnp.broadcast_to(ai[:, c0 + j : c0 + j + 1], (8, 128))
            ua = m * ra[j] if j == 0 else ua + m * ra[j]
            uw = m * rw[j] if j == 0 else uw + m * rw[j]
        a_ref[q, :] = ai - ua
        w_ref[q, :] = w_ref[q, :] - uw
    w_ref[c0 : c0 + 8, :] = wt


def kernel(
    m_hbm, g_hbm, q_hbm, mn, lf, back,
    mv, gv, qv, buf, mt, pp, sibr, rsr, pf, ph, plo, bp,
    run, solo, bfull, bh, bl, gl, gr, gt, ha, hp, ht, pt, g, li, wd, lh, ll, oh, bb, nsq, nr, nt, nz,
    in_s, s1s, s1r, s2s, s2r, s3s, s3r, s4s, s4r,
    gzs, gzr, gbs, gbr, gps, gpr, gss, gsr, has, har, hbs, hbr, nzs, nzr,
    ring_s, run_r, solo_r, all_r, skip_r, ns, nrs,
):
    z = lax.axis_index("row")
    c = lax.axis_index("col")
    y, x, k = c // 8, (c // 2) % 4, c % 2
    chip = y * NX + x
    mine = k * CHIPS + chip

    def dev(zz, yy, xx, kk):
        return (zz, (yy * NX + xx) * 2 + kk)

    def plane(dy, dx, kk):
        return dev(z, (y + dy) % NY, (x + dx) % NX, kk)

    def peer_chip(dy, dx):
        return ((y + dy) % NY) * NX + (x + dx) % NX

    offs = [(dy, dx) for dy in range(NY) for dx in range(NX) if dy or dx]
    sib = dev(z, y, x, 1 - k)

    def rcopy(src, dst, ss, rs, device):
        cp = pltpu.make_async_remote_copy(
            src_ref=src, dst_ref=dst, send_sem=ss, recv_sem=rs, device_id=device, device_id_type=MESH
        )
        cp.start()

    finals = []

    def wait_for(ref, sem):
        pltpu.make_async_copy(ref, ref, sem).wait()

    loads = [pltpu.make_async_copy(a, b, in_s.at[i]) for i, (a, b) in enumerate([(m_hbm, mv), (g_hbm, gv), (q_hbm, qv)])]
    for cp in loads:
        cp.start()

    bar = pltpu.get_barrier_semaphore()
    pl.semaphore_signal(bar, inc=1, device_id=sib, device_id_type=MESH)
    for dy, dx in offs:
        for kk in range(2):
            pl.semaphore_signal(bar, inc=1, device_id=plane(dy, dx, kk), device_id_type=MESH)
    for dz in range(1, NZ):
        pl.semaphore_signal(bar, inc=1, device_id=dev((z + dz) % NZ, y, x, k), device_id_type=MESH)

    my_half = pl.multiple_of(HALF * k, HALF)
    other_half = pl.multiple_of(HALF * (1 - k), HALF)
    my_piece = pl.multiple_of(HALF * k + PIECE * chip, PIECE)

    def project(start):
        rows = pl.ds(start, HALF)
        part = dot1(buf[rows, :], qv[...], NN)
        for q in range(CH):
            pp[q, rows, :] = part[:, LW * q : LW * q + LW]

    loads[0].wait()
    loads[1].wait()
    for r in range(4):
        rows = pl.ds(128 * r, 128)
        buf[rows, :] = (mv[rows, :].astype(F32) + gv[rows, :].astype(F32)).astype(BF16)
    loads[2].wait()
    project(other_half)

    pl.semaphore_wait(bar, 31 + NZ - 1)

    for q in range(CH):
        rcopy(pp.at[q, pl.ds(other_half, HALF)], sibr.at[q], s1s.at[q], s1r.at[q], sib)
        finals.append(lambda q=q: wait_for(sibr.at[q], s1s.at[q]))
    project(my_half)
    for q in range(CH):
        wait_for(sibr.at[q], s1r.at[q])
        rows = pl.ds(my_half, HALF)
        pp[q, rows, :] = pp[q, rows, :] + sibr[q]
        for n, (dy, dx) in enumerate(offs):
            piece = pl.multiple_of(HALF * k + PIECE * peer_chip(dy, dx), PIECE)
            rcopy(pp.at[q, pl.ds(piece, PIECE)], rsr.at[q, n], s2s.at[q], s2r.at[q], plane(dy, dx, k))
    for r in range(4):
        mt[:, 128 * r : 128 * r + 128] = buf[128 * r : 128 * r + 128, :].T
    for q in range(CH):
        finals.append(lambda q=q: wait_for(rsr.at[q], s2s.at[q]))
        finals.append(lambda q=q: wait_for(rsr.at[q], s3s.at[q]))
        wait_for(rsr.at[q], s2r.at[q])
        rows = pl.ds(my_piece, PIECE)
        total = pp[q, rows, :]
        for n in range(CHIPS - 1):
            total = total + rsr[q, n]
        pf[q, rows, :] = total
        for n, (dy, dx) in enumerate(offs):
            rcopy(pf.at[q, rows], pf.at[q, rows], s3s.at[q], s3r.at[q], plane(dy, dx, k))
    for q in range(CH):
        wait_for(rsr.at[q], s3r.at[q])
        half = pf.at[q, pl.ds(my_half, HALF)]
        rcopy(half, half, s4s.at[q], s4r.at[q], sib)
        finals.append(lambda q=q: wait_for(sibr.at[q], s4s.at[q]))

    def shard(i):
        return pl.ds(pl.multiple_of(SH * lax.rem(i + 2 * NZ, NZ), 8), SH)

    def zdev(step):
        return dev((z + step + NZ) % NZ, y, x, k)

    def ring_events(q):
        sent = [0, 0]

        def send(src, dst, way, sem, hop):
            sent[way] += 1
            rcopy(src, dst, ring_s.at[q, way], sem, zdev(hop if way == 0 else -hop))

        def at(way, dist):
            return shard(z + dist if way == 0 else z - dist)

        def finish(way):
            def fn():
                for n in range(0, sent[way], NZ):
                    wait_for(bfull.at[q, pl.ds(0, SH * min(NZ, sent[way] - n))], ring_s.at[q, way])
            return fn

        finals.append(finish(0))
        finals.append(finish(1))
        hops = [len(PLANS[q][0]) - 1, len(PLANS[q][1]) - 1]
        for way in range(2):
            stops = PLANS[q][way]
            send(bp.at[q, at(way, stops[0])], run.at[q, way, 0], way, run_r.at[q, way, 0], stops[0] - stops[1])

        def solos():
            for way in range(2):
                stops = PLANS[q][way]
                for i in range(hops[way]):
                    if stops[i] - stops[i + 1] == 2:
                        send(bp.at[q, at(way, stops[i] - 1)], solo.at[q, way, i], way, solo_r.at[q, way, i], 1)

        yield

        def arrived(way, i):
            stops = PLANS[q][way]
            wait_for(run.at[q, way, i], run_r.at[q, way, i])
            total = run[q, way, i]
            if stops[i] - stops[i + 1] == 2:
                wait_for(solo.at[q, way, i], solo_r.at[q, way, i])
                total = total + solo[q, way, i]
            return total

        for i in range(1, max(hops)):
            for way in range(2):
                stops = PLANS[q][way]
                if i < hops[way]:
                    run[q, way, i - 1] = arrived(way, i - 1) + bp[q, at(way, stops[i]), :]
                    send(run.at[q, way, i - 1], run.at[q, way, i], way, run_r.at[q, way, i], stops[i] - stops[i + 1])
            if i == 1 + q:
                solos()
            yield
        own = shard(z)
        total = arrived(0, hops[0] - 1) + arrived(1, hops[1] - 1)
        bfull[q, own, :] = bp[q, own, :] + total

        def forward(way, i):
            stops = PLANS[q][way][::-1]
            blk = bfull.at[q, at(way, -stops[i])]
            if i:
                wait_for(blk, all_r.at[q, way, i - 1])
            if i < hops[way]:
                send(blk, blk, way, all_r.at[q, way, i], stops[i + 1] - stops[i])

        def skips(way, i):
            stops = PLANS[q][way][::-1]
            if 0 <= i < hops[way] and stops[i + 1] - stops[i] == 2:
                blk = bfull.at[q, at(way, -stops[i])]
                send(blk, blk, way, skip_r.at[q, way, i], 1)

        for i in range(max(hops) + 1):
            for way in range(2):
                if i <= hops[way]:
                    forward(way, i)
            for way in range(2):
                skips(way, i - 1 - q)
            if i == max(hops):
                for way in range(2):
                    stops = PLANS[q][way][::-1]
                    for n in range(hops[way]):
                        if stops[n + 1] - stops[n] == 2:
                            wait_for(bfull.at[q, at(way, -stops[n] - 1)], skip_r.at[q, way, n])
            yield

    events = []
    for q in range(CH):
        wait_for(sibr.at[q], s4r.at[q])
        high, low = split(pf[q])
        cols = slice(LW * q, LW * q + LW)
        ph[:, cols] = high
        plo[:, cols] = low
        both = jnp.concatenate([high, low], axis=1)
        for r in range(7):
            rows = pl.ds(128 * r, 128)
            part = dot1(mt[rows, :], both, NN)
            bp[q, rows, :] = part[:, :128] + part[:, 128:]
        events.append(ring_events(q))
        next(events[q])
        pt[cols, :] = pf[q].T
        if q == 0:
            @pl.when(k == 0)
            def _():
                ha[...] = doth(pt[pl.ds(pl.multiple_of(8 * chip, 8), 8), :], pf[0], NN)
                for dz in range(1, NZ):
                    rcopy(ha, hp.at[z], has, har, dev((z + dz) % NZ, y, x, k))

    my_u = (z % 8) * 3 % 8
    owner = my_u < OWN
    my_u = my_u % OWN
    my_tiles = OWN * mine

    eye = lax.broadcasted_iota(jnp.int32, (128, 128), 0) == lax.broadcasted_iota(jnp.int32, (128, 128), 1)

    def head():
        @pl.when(k == 0)
        def _():
            wait_for(hp.at[pl.ds(0, NZ - 1)], har)
            hp[z] = ha[...]
            total = hp[0]
            for n in range(1, NZ):
                total = total + hp[n]
            ht[chip] = total
            tile = ht.at[chip]
            rcopy(tile, tile, hbs, hbr, sib)
            for dy, dx in offs:
                for kk in range(2):
                    rcopy(tile, tile, hbs, hbr, plane(dy, dx, kk))

        def done_sending():
            @pl.when(k == 0)
            def _():
                wait_for(gt.at[pl.ds(0, NZ - 1)], has)
                wait_for(gt.at[pl.ds(0, 31)], hbs)

        finals.append(done_sending)
        yield

        @pl.when(k == 0)
        def _():
            wait_for(gt.at[pl.ds(0, CHIPS - 1)], hbr)

        @pl.when(k == 1)
        def _():
            wait_for(gt.at[pl.ds(0, CHIPS)], hbr)

        g[:128, :128] = ht[...].reshape(128, 128)
        wd[...] = eye.astype(F32)
        yield
        for t in range(16):
            leaf(g.at[:128, :128], wd, t)
            yield

    def chol():
        for u in range(OWN):
            tile = my_tiles + u
            b = tile // 16
            i = (b + 9) // 10 + (b + 7) // 10 + (b + 4) // 10
            j = b - i * (i + 1) // 2
            lhs = pt[pl.ds(pl.multiple_of(128 * i + 8 * (tile % 16), 8), 8), :]
            gl[u] = doth(lhs, pf[j], NN)
        for u in range(OWN):
            for far in (0, 8):
                at_z = (3 * u + far) % NZ

                @pl.when(z != at_z)
                def _():
                    rcopy(gl.at[u], gr.at[z], gzs, gzr, dev(at_z, y, x, k))

        def f1():
            @pl.when(owner)
            def _():
                wait_for(gt.at[pl.ds(0, 2 * OWN - 1)], gzs)
                wait_for(gt.at[pl.ds(0, 7)], gbs)

            @pl.when(jnp.logical_not(owner))
            def _():
                wait_for(gt.at[pl.ds(0, 2 * OWN)], gzs)

        finals.append(f1)
        finals.append(lambda: wait_for(gt.at[pl.ds(0, OWN * (CHIPS - 1))], gps))
        finals.append(lambda: wait_for(gt.at[pl.ds(0, OWN * CHIPS)], gss))
        yield
        @pl.when(owner)
        def _():
            wait_for(gr.at[pl.ds(0, NZ - 1)], gzr)
            gr[z] = gl[my_u]
            total = gr[0]
            for n in range(1, NZ):
                total = total + gr[n]
            dst = gt.at[my_tiles + my_u]
            gt[my_tiles + my_u] = total
            for dz in (1, -1, 2, -2, 3, -3, 4):
                rcopy(dst, dst, gbs, gbr, dev((z + dz + NZ) % NZ, y, x, k))
        yield
        own = gt.at[pl.ds(my_tiles, OWN)]
        @pl.when(owner)
        def _():
            wait_for(gt.at[pl.ds(0, OWN - 1)], gbr)
        @pl.when(jnp.logical_not(owner))
        def _():
            wait_for(gt.at[pl.ds(0, OWN)], gbr)
        for n, (dy, dx) in enumerate(offs):
            rcopy(own, own, gps, gpr, plane(dy, dx, k))
        yield
        wait_for(gt.at[pl.ds(0, OWN * (CHIPS - 1))], gpr)
        half = gt.at[pl.ds(OWN * CHIPS * k, OWN * CHIPS)]
        rcopy(half, half, gss, gsr, sib)
        yield
        wait_for(gt.at[pl.ds(0, OWN * CHIPS)], gsr)
        for b, (i, j) in enumerate(BLOCKS[1:], 1):
            g[128 * i : 128 * i + 128, 128 * j : 128 * j + 128] = gt[16 * b : 16 * b + 16].reshape(128, 128)
        yield
        yield from first
        for kb in range(4):
            K = slice(128 * kb, 128 * kb + 128)
            before = slice(0, 128 * kb)
            if kb:
                wd[...] = eye.astype(F32)
                for t in range(16):
                    leaf(g.at[K, K], wd, t)
                    yield
            w = wd[...]
            li[K, K] = w
            if kb:
                li[K, before] = doth(w, li[K, before], NN)
            if kb < 3:
                R = slice(128 * (kb + 1), 512)
                lp = doth(g[R, K], w, NT)
                g[R, R] = g[R, R] - doth(lp, lp, NT)
                yield
                if kb:
                    li[R, before] = li[R, before] - doth(lp, li[K, before], NN)
                li[R, K] = -doth(lp, w, NN)
                li[K, 128 * (kb + 1) :] = jnp.zeros((128, 512 - 128 * (kb + 1)), F32)
            yield
        lh[...], ll[...] = split(li[...])
        own = pl.ds(pl.multiple_of(SH * z, 8), SH)
        high, low = split(jnp.concatenate([bfull[q, own, :] for q in range(CH)], axis=1))
        part = dot1(high, lh[...], NT) + (dot1(high, ll[...], NT) + dot1(low, lh[...], NT))
        sq = jnp.sum(part * part, axis=0, keepdims=True)
        for q in range(CH):
            nsq[q : q + 1, :] = sq[:, 128 * q : 128 * q + 128]
        finals.append(lambda: wait_for(nr, ns))
        rcopy(nsq, nr.at[0], ns, nrs, sib)
        for n, (dy, dx) in enumerate(offs):
            for kk in range(2):
                rcopy(nsq, nr.at[1 + 2 * n + kk], ns, nrs, plane(dy, dx, jnp.where(kk == 0, k, 1 - k)))
        yield
        for h in range(2):
            J = slice(256 * h, 256 * h + 256)
            K = 256 * (h + 1)
            a, b = lh[J, :K], ll[J, :K]
            orth = dot1(ph[:, :K], a, NT) + (dot1(ph[:, :K], b, NT) + dot1(plo[:, :K], a, NT))
            oh[:, J] = orth.astype(BF16)
            lf[:, J] = jnp.sqrt(F32(NZ * ROWS_L)) * orth
            yield
        for _ in range(PER_GAP * NORM_GAPS - 2):
            yield
        wait_for(nr, nrs)
        total = nsq[...]
        for n in range(31):
            total = total + nr[n]
        nt[...] = total
        finals.append(lambda: wait_for(nz.at[pl.ds(0, NZ - 1)], nzs))
        for dz in range(1, NZ):
            rcopy(nt, nz.at[z], nzs, nzr, dev((z + dz) % NZ, y, x, k))
        yield

    first = head()
    work = chol()
    done = object()

    def pull(n):
        for _ in range(n):
            next(work, done)

    pull(1)
    def products(rows, cols):
        for q in range(cols.start // LW, cols.stop // LW):
            J = slice(LW * q, LW * q + LW)
            bh[:, J], bl[:, J] = split(bfull[q])
        a, b = lh[rows, cols], ll[rows, cols]
        return dot1(bh[:, cols], a, NT) + (dot1(bh[:, cols], b, NT) + dot1(bl[:, cols], a, NT))

    def apply_early():
        while next(work, done) is not done:
            pass
        part = products(slice(0, 512), slice(0, 256))
        back[...] = part
        bb[:, :256] = part[:, :256].astype(BF16)

    def apply_late():
        part = back[:, 256:] + products(slice(256, 512), slice(256, 512))
        back[:, 256:] = part
        bb[:, 256:] = part.astype(BF16)

    last = max(len(p) - 1 for plan in PLANS for p in plan) * 2
    count = 0
    for e in range(1, last + 1):
        for q in range(CH):
            if e == last and q == 2:
                apply_early()
            if next(events[q], done) is done:
                continue
            count += 1
            if count in GRAM_AT:
                pull(1)
            elif count > GRAM_AT[-1]:
                pull(PER_GAP)
            if count in HEAD_AT or HEAD_AT[-1] < count < GRAM_AT[-1]:
                next(first, done)
    apply_late()
    for first in range(0, COLS_L, 256):
        cols = slice(first, min(first + 256, COLS_L))
        update = dot1(oh[...], bb[cols, :], NT)
        mn[:, cols] = (buf[:, cols].astype(F32) - F32(1.0 - decay) * update).astype(BF16)

    wait_for(nz.at[pl.ds(0, NZ - 1)], nzr)
    nz[z] = nt[...]
    total = nz[0]
    for n in range(1, NZ):
        total = total + nz[n]
    scale = jnp.sqrt(F32(2 * CHIPS * COLS_L)) * lax.rsqrt(total + 1e-06)
    for q in range(CH):
        J = slice(128 * q, 128 * q + 128)
        back[:, J] = back[:, J] * scale[q : q + 1, :]

    for fn in finals:
        fn()


def finish(mom, left, right, mom_out, left_out, right_out, sems):
    pairs = [(right, right_out), (left, left_out), (mom, mom_out)]
    copies = [pltpu.make_async_copy(a, b, sems.at[n]) for n, (a, b) in enumerate(pairs)]
    for cp in copies:
        cp.start()
    for cp in copies:
        cp.wait()


def shards(momentum, gradient, basis):
    V = pltpu.VMEM
    D = pltpu.SemaphoreType.DMA
    scratch = [
        V((512, 896), BF16), V((512, 896), BF16), V((896, 512), BF16),
        V((512, 896), BF16), V((896, 512), BF16),
        V((CH, 512, 128), F32), V((CH, HALF, 128), F32), V((CH, CHIPS - 1, PIECE, 128), F32),
        V((CH, 512, 128), F32), V((512, 512), BF16), V((512, 512), BF16), V((CH, 896, 128), F32),
        V((CH, 2, 8, SH, 128), F32), V((CH, 2, 8, SH, 128), F32), V((CH, 896, 128), F32),
        V((896, 512), BF16), V((896, 512), BF16),
        V((OWN, 8, 128), F32), V((NZ, 8, 128), F32), V((TILES, 8, 128), F32),
        V((8, 128), F32), V((NZ, 8, 128), F32), V((16, 8, 128), F32),
        V((512, 512), F32), V((512, 512), F32), V((512, 512), F32), V((128, 128), F32),
        V((512, 512), BF16), V((512, 512), BF16), V((512, 512), BF16),
        V((896, 512), BF16), V((4, 128), F32), V((31, 4, 128), F32), V((4, 128), F32), V((NZ, 4, 128), F32),
        D((3,)), D((CH,)), D((CH,)), D((CH,)), D((CH,)), D((CH,)), D((CH,)), D((CH,)), D((CH,)),
        D, D, D, D, D, D, D, D, D, D, D, D, D, D,
        D((CH, 2)), D((CH, 2, 8)), D((CH, 2, 8)), D((CH, 2, 8)), D((CH, 2, 8)), D, D,
    ]
    results = pl.pallas_call(
        kernel,
        name="dion",
        out_shape=(
            pltpu.VMEM((512, 896), BF16),
            pltpu.VMEM((512, 512), F32),
            pltpu.VMEM((896, 512), F32),
        ),
        in_specs=[pl.BlockSpec(memory_space=pltpu.HBM)] * 3,
        out_specs=[pl.BlockSpec(memory_space=pltpu.VMEM)] * 3,
        scratch_shapes=scratch,
        compiler_params=pltpu.CompilerParams(
            collective_id=0, has_side_effects=True, vmem_limit_bytes=40 * 2**20
        ),
    )(*[pltpu.with_memory_space_constraint(a, pltpu.HBM) for a in (momentum, gradient, basis)])
    return pl.pallas_call(
        finish,
        name="finish",
        out_shape=(
            jax.ShapeDtypeStruct((512, 896), BF16),
            jax.ShapeDtypeStruct((512, 512), F32),
            jax.ShapeDtypeStruct((896, 512), F32),
        ),
        in_specs=[pl.BlockSpec(memory_space=pl.ANY)] * 3,
        out_specs=[pl.BlockSpec(memory_space=pl.ANY)] * 3,
        scratch_shapes=[D((3,))],
        compiler_params=pltpu.CompilerParams(vmem_limit_bytes=4 * 2**20),
    )(*results)


def solution(mesh):
    in_specs = (P("row", "col"), P("row", "col"), P("col", None))
    out_specs = (P("row", "col"), P("row", None), P("col", None))
    return jax.shard_map(shards, mesh=mesh, in_specs=in_specs, out_specs=out_specs, check_vma=False)
```
